32 devices in a mesh: groups: 2 (over x), seq: 16 (over z, y, core).
Axes of the slice: x: 2, y: 2, z: 4, core: 2. Of those that a mesh axis runs over, the one named last changes fastest.
Arguments:
- queries: bfloat16 [12288, 2048], P(('groups', 'seq')), parts along dimension 0, may hold values from -6 to 6
- keys: bfloat16 [12288, 2048], P(('groups', 'seq')), parts along dimension 0, may hold values from -6 to 6
- values: bfloat16 [12288, 2048], P(('groups', 'seq')), parts along dimension 0, may hold values from -6 to 6
- out_grad: bfloat16 [12288, 2048], P(('groups', 'seq')), parts along dimension 0, may hold values from -6 to 6
Outputs:
- relaid: bfloat16 [16, 12288, 128], P('seq', 'groups'), parts along dimension 1
- query_grad: bfloat16 [12288, 2048], P(('groups', 'seq')), parts along dimension 0
- key_grad: bfloat16 [12288, 2048], P(('groups', 'seq')), parts along dimension 0
- value_grad: bfloat16 [12288, 2048], P(('groups', 'seq')), parts along dimension 0
The draws below stay inside these ranges and needn't reach their ends.
There are 2 independent parts, one for each index of `groups`. The reference program is written for one: setup_inputs(seed, part) draws one part's arguments, and reference() takes and returns one part's arrays. A program takes and returns all parts, laid end to end along the dimension named above; each array names one. Nothing has to cross between parts.
All inputs are finite; a program needn't handle non-finite values.
Results may differ from the reference program's by a relative error of at most 0.0058.
Values may be sent and summed in bfloat16 or wider, within the bound.
A program may use at most 128 MiB of HBM per device.

```python
import jax
import jax.numpy as jnp
from jax import lax

H = 16
DH = 128
TOK_DEV = 384
D = 2048
TOKENS = 6144
SPLITS = 1
PIECE = 384
N_SEQ = 16


def levels(rng, extent, cuts, low, high):
    loudness = 1.0
    for position, shards_of in cuts:
        heights = jax.random.uniform(jax.random.fold_in(jax.random.fold_in(rng, 6), position), (shards_of,), jnp.float32, low / len(cuts), high / len(cuts))
        loudness = loudness * jnp.repeat(jnp.exp(heights), extent[position] // shards_of).reshape((-1,) + (1,) * (len(extent) - 1 - position))
    return loudness


def normal_values(own_key, shape, spread, most, cuts=(), kind=jnp.bfloat16):
    level = levels(own_key, shape, cuts, -0.22, 0.18) if cuts else 1.0
    drawn = jax.random.normal(own_key, shape, jnp.float32) * spread * level
    return jnp.minimum(jnp.maximum(drawn, -most), most).astype(kind)


def setup_inputs(seed: int = 0, part: int = 0) -> dict:
    streams_of = jax.random.split(jax.random.key(seed), 5)
    part_keys = jax.random.split(jax.random.fold_in(streams_of[4], part), 5)
    return {
        "queries": normal_values(part_keys[0], (TOKENS, D), 1.0, 6.0, ((0, 16),)),
        "keys": normal_values(part_keys[1], (TOKENS, D), 1.0, 6.0, ((0, 16),)),
        "values": normal_values(part_keys[2], (TOKENS, D), 1.0, 6.0, ((0, 16),)),
        "out_grad": normal_values(part_keys[3], (TOKENS, D), 1.0, 6.0, ((0, 16),)),
    }


eps = 1e-06

def causal_mask(count):
    rows = lax.broadcasted_iota(jnp.int32, (count, count), 0)
    cols = lax.broadcasted_iota(jnp.int32, (count, count), 1)
    return rows >= cols

def block_values(q, k, v, state_b, mask):
    qf = q.astype(jnp.float32)
    kf = k.astype(jnp.float32)
    vf = v.astype(jnp.float32)
    scores = jnp.einsum('thd,shd->hts', qf, kf)
    masked = jnp.where(mask[None], scores, 0.0).astype(jnp.bfloat16)
    intra = jnp.einsum('hts,shd->thd', masked.astype(jnp.float32), vf)
    inter = jnp.einsum('thd,hde->the', qf, state_b.astype(jnp.float32))
    acc = intra + inter
    norm = jnp.sqrt(lax.optimization_barrier(jnp.mean(acc * acc, axis=-1, keepdims=True)) + eps)
    return (masked, acc, norm)

def reference(queries, keys, values, out_grad):
    shape4 = (N_SEQ, TOK_DEV, H, DH)
    q_blocks = queries.reshape(shape4)
    k_blocks = keys.reshape(shape4)
    v_blocks = values.reshape(shape4)
    g_blocks = out_grad.reshape(shape4)
    mask = causal_mask(TOK_DEV)
    zero = jnp.zeros((H, DH, DH), jnp.float32)

    def forward(state, block):
        q, k, v = block
        state_b = state.astype(jnp.bfloat16)
        masked, acc, norm = block_values(q, k, v, state_b, mask)
        out = (acc / norm).astype(jnp.bfloat16)
        new_state = state + jnp.einsum('shd,she->hde', k.astype(jnp.float32), v.astype(jnp.float32))
        return (new_state, (out, state_b))
    final_state, (outs, states) = lax.scan(forward, zero, (q_blocks, k_blocks, v_blocks))

    def backward(later, block):
        q, k, v, g, state_b = block
        masked, acc, norm = block_values(q, k, v, state_b, mask)
        qf = q.astype(jnp.float32)
        kf = k.astype(jnp.float32)
        vf = v.astype(jnp.float32)
        unit = acc / norm
        gf = g.astype(jnp.float32)
        inner = lax.optimization_barrier(jnp.mean(gf * unit, axis=-1, keepdims=True))
        d_acc = ((gf - unit * inner) / norm).astype(jnp.bfloat16)
        daf = d_acc.astype(jnp.float32)
        dscore = jnp.einsum('thd,shd->hts', daf, vf)
        dscore = jnp.where(mask[None], dscore, 0.0).astype(jnp.bfloat16).astype(jnp.float32)
        later_b = later.astype(jnp.bfloat16).astype(jnp.float32)
        state_f = state_b.astype(jnp.float32)
        dq = jnp.einsum('hts,shd->thd', dscore, kf) + jnp.einsum('the,hde->thd', daf, state_f)
        dk = jnp.einsum('hts,thd->shd', dscore, qf) + jnp.einsum('she,hde->shd', vf, later_b)
        dv = jnp.einsum('hts,the->she', masked.astype(jnp.float32), daf) + jnp.einsum('shd,hde->she', kf, later_b)
        new_later = later + jnp.einsum('thd,the->hde', qf, daf)
        return (new_later, (dq.astype(jnp.bfloat16), dk.astype(jnp.bfloat16), dv.astype(jnp.bfloat16)))
    first_later, (dq, dk, dv) = lax.scan(backward, zero, (q_blocks, k_blocks, v_blocks, g_blocks, states), reverse=True)
    pieces = outs.reshape(N_SEQ, SPLITS, PIECE, H, DH)
    relaid = jnp.transpose(pieces, (1, 3, 0, 2, 4)).reshape(SPLITS * H, N_SEQ * PIECE, DH)
    return (relaid, dq.reshape(TOKENS, D), dk.reshape(TOKENS, D), dv.reshape(TOKENS, D))
```

```python
import functools

import jax
import jax.numpy as jnp
from jax import lax
from jax.experimental import pallas as pl
from jax.experimental.pallas import tpu as pltpu
from jax.sharding import PartitionSpec as P

DH = 128
EPS = 1e-06
F32 = jnp.float32
BF16 = jnp.bfloat16
WIRE_LOCAL = jnp.bfloat16
WIRE_PLANE = jnp.bfloat16


def dot(a, b, ca, cb):
    return lax.dot_general(a, b, (((ca,), (cb,)), ((), ())), preferred_element_type=F32)


def remote(src, dst, send_sem, recv_sem, device):
    return pltpu.make_async_remote_copy(
        src_ref=src,
        dst_ref=dst,
        send_sem=send_sem,
        recv_sem=recv_sem,
        device_id={"seq": device},
        device_id_type=pl.DeviceIdType.MESH,
    )


class Scan:
    def __init__(self, me, planes, members, share, forward, bufs):
        (self.mine, self.states, self.total, self.run, self.out2, self.in2, self.out3,
         self.result, self.s1, self.r1, self.s2, self.r2, self.s3, self.r3) = bufs
        self.planes, self.members, self.share, self.forward = planes, members, share, forward
        self.z, self.j = me // members, me % members
        self.zz = self.z if forward else planes - 1 - self.z
        self.levels = planes.bit_length() - 1

    def push(self, h, value):
        o, i = h // self.share, h % self.share

        @pl.when(o == self.j)
        def _():
            self.states[i, self.j] = value.astype(self.states.dtype)

        @pl.when(o != self.j)
        def _():
            self.mine[h] = value.astype(self.mine.dtype)
            remote(self.mine.at[h], self.states.at[i, self.j], self.s1.at[h],
                   self.r1.at[i, self.j], self.z * self.members + o).start()

    def plane_device(self, zz):
        z = zz if self.forward else self.planes - 1 - zz
        return z * self.members + self.j

    def sends(self, level):
        return (self.zz & ((2 << level) - 1)) == (1 << level) - 1

    def up(self, level, i, d):
        return remote(self.out2.at[level, i], self.in2.at[level, i], self.s2.at[level, d, i],
                      self.r2.at[level, i], self.plane_device(self.zz + 1 + d))

    def start_level(self, level, i):
        @pl.when(self.sends(level))
        def _():
            value = self.total[i] if level == 0 else self.run[i] + self.total[i]
            self.out2[level, i] = value.astype(self.out2.dtype)
            for d in range(1 << level):
                self.up(level, i, d).start()

    def gather(self):
        for i in range(self.share):
            for s in range(1, self.members):
                o = self.j ^ s
                remote(self.mine.at[0], self.states.at[i, o], self.s1.at[0], self.r1.at[i, o],
                       self.z * self.members + o).wait_recv()
            total = self.states[i, 0].astype(F32)
            for o in range(1, self.members):
                total += self.states[i, o].astype(F32)
            self.total[i] = total
            self.run[i] = jnp.zeros_like(total)
            self.start_level(0, i)

    def spread(self):
        for i in range(self.share):
            for level in range(self.levels):
                if level:
                    self.start_level(level, i)

                @pl.when(((self.zz >> level) & 1) == 1)
                def _():
                    self.up(level, i, 0).wait_recv()
                    self.run[i] += self.in2[level, i].astype(F32)

            total = self.run[i]
            order = range(self.members) if self.forward else range(self.members - 1, -1, -1)
            h = self.j * self.share + i
            for o in order:
                rounded = total.astype(BF16)
                total += self.states[i, o].astype(F32)

                @pl.when(o == self.j)
                def _():
                    self.result[h] = rounded

                @pl.when(o != self.j)
                def _():
                    self.out3[i, o] = rounded
                    remote(self.out3.at[i, o], self.result.at[h], self.s3.at[i, o],
                           self.r3.at[h], self.z * self.members + o).start()

    def take(self, h):
        o = h // self.share

        @pl.when(o != self.j)
        def _():
            remote(self.out3.at[0, 0], self.result.at[h], self.s3.at[0, 0], self.r3.at[h],
                   self.z * self.members + o).wait_recv()

    def drain(self):
        for i in range(self.share):
            for s in range(1, self.members):
                o = self.j ^ s
                h = o * self.share + i
                remote(self.mine.at[h], self.states.at[i, self.j], self.s1.at[h],
                       self.r1.at[i, self.j], self.z * self.members + o).wait_send()
                remote(self.out3.at[i, o], self.result.at[h], self.s3.at[i, o], self.r3.at[h],
                       self.z * self.members + o).wait_send()
            for level in range(self.levels):
                @pl.when(self.sends(level))
                def _():
                    for d in range(1 << level):
                        self.up(level, i, d).wait_send()


def kernel(n, members, q_hbm, k_hbm, v_hbm, g_hbm, relaid, dq_hbm, dk_hbm, dv_hbm,
           q_ref, k_ref, v_ref, g_ref, dq_ref, dk_ref, dv_ref, score, intra, out, d_acc,
           dk_part, dv_part, in_sem, out_sem, own_sem, relaid_send, relaid_recv, *scans):
    me = lax.axis_index("seq")
    rows, width = q_ref.shape
    heads = width // DH
    planes, share = n // members, heads // members
    pieces = n // heads
    piece = rows // pieces
    fwd = Scan(me, planes, members, share, True, scans[: len(scans) // 2])
    bwd = Scan(me, planes, members, share, False, scans[len(scans) // 2:])

    loads = [
        pltpu.make_async_copy(src, dst, in_sem.at[x])
        for x, (src, dst) in enumerate(
            ((k_hbm, k_ref), (v_hbm, v_ref), (q_hbm, q_ref), (g_hbm, g_ref)))
    ]
    for load in loads:
        load.start()
    barrier = pltpu.get_barrier_semaphore()

    def greet(s, carry):
        pl.semaphore_signal(barrier, inc=1, device_id={"seq": lax.rem(me + s, n)},
                            device_id_type=pl.DeviceIdType.MESH)
        return carry

    lax.fori_loop(1, n, greet, 0)

    def cols(h):
        return pl.ds(pl.multiple_of(h * DH, DH), DH)

    loads[0].wait()
    loads[1].wait()
    pl.semaphore_wait(barrier, n - 1)

    def local_step(t, carry):
        h = (fwd.j ^ (members - 1 - t % members)) * share + t // members
        fwd.push(h, dot(k_ref[:, cols(h)], v_ref[:, cols(h)], 0, 0))
        return carry

    lax.fori_loop(0, heads, local_step, 0)
    loads[2].wait()
    causal = (lax.broadcasted_iota(jnp.int32, (rows, rows), 0)
              >= lax.broadcasted_iota(jnp.int32, (rows, rows), 1))

    def intra_step(h, carry):
        s = dot(q_ref[:, cols(h)], k_ref[:, cols(h)], 1, 1)
        s = jnp.where(causal, s, 0.0).astype(BF16)
        score[h] = s
        intra[h] = dot(s, v_ref[:, cols(h)], 1, 0)
        return carry

    lax.fori_loop(0, heads, intra_step, 0)
    loads[3].wait()
    fwd.gather()
    fwd.spread()

    def relaid_copy(h, p):
        return remote(out.at[h, pl.ds(p * piece, piece)],
                      relaid.at[0, pl.ds(pl.multiple_of(me * piece, 16), piece)],
                      relaid_send, relaid_recv, p * heads + h)

    def own_copy(p):
        return pltpu.make_async_copy(
            out.at[me % heads, pl.ds(pl.multiple_of(p * piece, 16), piece)],
            relaid.at[0, pl.ds(pl.multiple_of(me * piece, 16), piece)], own_sem)

    def main_step(t, carry):
        h = (((me // members) % members) ^ (members - 1 - t % members)) * share + t // members
        fwd.take(h)
        q = q_ref[:, cols(h)]
        acc = intra[h] + dot(q, fwd.result[h], 1, 0)
        inv = lax.rsqrt(jnp.mean(acc * acc, axis=-1, keepdims=True) + EPS)
        unit = acc * inv
        out[h] = unit.astype(BF16)
        for p in range(pieces):
            @pl.when(p * heads + h != me)
            def _():
                relaid_copy(h, p).start()
        g = g_ref[:, cols(h)].astype(F32)
        inner = jnp.mean(g * unit, axis=-1, keepdims=True)
        da = ((g - unit * inner) * inv).astype(BF16)
        d_acc[h] = da
        bwd.push(h, dot(q, da, 0, 0))
        return carry

    lax.fori_loop(0, heads, main_step, 0)
    own_copy(me // heads).start()

    def grad_step(h, carry):
        q, k, v = q_ref[:, cols(h)], k_ref[:, cols(h)], v_ref[:, cols(h)]
        da = d_acc[h]
        ds = dot(da, v, 1, 1)
        ds = jnp.where(causal, ds, 0.0).astype(BF16)
        dq_ref[:, cols(h)] = (dot(ds, k, 1, 0) + dot(da, fwd.result[h], 1, 1)).astype(BF16)
        dk_part[h] = dot(ds, q, 0, 0)
        dv_part[h] = dot(score[h], da, 0, 0)
        return carry

    lax.fori_loop(0, heads, grad_step, 0)
    dq_out = pltpu.make_async_copy(dq_ref, dq_hbm, out_sem.at[0])
    dq_out.start()
    bwd.gather()
    bwd.spread()

    def last_step(t, carry):
        h = (t % members) * share + t // members
        bwd.take(h)
        later = bwd.result[h]
        dk_ref[:, cols(h)] = (dk_part[h] + dot(v_ref[:, cols(h)], later, 1, 1)).astype(BF16)
        dv_ref[:, cols(h)] = (dv_part[h] + dot(k_ref[:, cols(h)], later, 1, 0)).astype(BF16)
        return carry

    lax.fori_loop(0, heads, last_step, 0)
    dk_out = pltpu.make_async_copy(dk_ref, dk_hbm, out_sem.at[1])
    dv_out = pltpu.make_async_copy(dv_ref, dv_hbm, out_sem.at[2])
    dk_out.start()
    dv_out.start()
    fwd.drain()
    bwd.drain()
    own_copy(me // heads).wait()
    whole = relaid.at[0, pl.ds(0, (n - 1) * piece)]
    pltpu.make_async_copy(whole, whole, relaid_send).wait()
    pltpu.make_async_copy(whole, whole, relaid_recv).wait()
    dq_out.wait()
    dk_out.wait()
    dv_out.wait()


def body(queries, keys, values, out_grad):
    n = lax.axis_size("seq")
    rows, width = queries.shape
    heads = width // DH
    members = min(heads, n // 4 if n <= heads else n // 8)
    planes, share = n // members, heads // members
    levels = planes.bit_length() - 1
    piece = rows * heads // n
    dma = pltpu.SemaphoreType.DMA
    state = (DH, DH)
    scan = [
        pltpu.VMEM((heads,) + state, WIRE_LOCAL),
        pltpu.VMEM((share, members) + state, WIRE_LOCAL),
        pltpu.VMEM((share,) + state, F32),
        pltpu.VMEM((share,) + state, F32),
        pltpu.VMEM((levels, share) + state, WIRE_PLANE),
        pltpu.VMEM((levels, share) + state, WIRE_PLANE),
        pltpu.VMEM((share, members) + state, BF16),
        pltpu.VMEM((heads,) + state, BF16),
        dma((heads,)),
        dma((share, members)),
        dma((levels, 1 << (levels - 1), share)),
        dma((levels, share)),
        dma((share, members)),
        dma((heads,)),
    ]
    by_head = (heads, rows, DH)
    any_space = pl.BlockSpec(memory_space=pl.ANY)
    return pl.pallas_call(
        functools.partial(kernel, n, members),
        out_shape=(
            jax.ShapeDtypeStruct((1, n * piece, DH), BF16),
            jax.ShapeDtypeStruct((rows, width), BF16),
            jax.ShapeDtypeStruct((rows, width), BF16),
            jax.ShapeDtypeStruct((rows, width), BF16),
        ),
        in_specs=[any_space] * 4,
        out_specs=(any_space,) * 4,
        scratch_shapes=[pltpu.VMEM((rows, width), BF16)] * 7
        + [
            pltpu.VMEM((heads, rows, rows), BF16),
            pltpu.VMEM(by_head, F32),
            pltpu.VMEM(by_head, BF16),
            pltpu.VMEM(by_head, BF16),
            pltpu.VMEM(by_head, F32),
            pltpu.VMEM(by_head, F32),
            dma((4,)),
            dma((3,)),
            dma,
            dma,
            dma,
        ]
        + scan
        + scan,
        compiler_params=pltpu.CompilerParams(
            collective_id=0, has_side_effects=True, vmem_limit_bytes=56 * 2**20
        ),
        cost_estimate=pl.CostEstimate(
            flops=heads * rows * DH * 12 * (rows + DH),
            bytes_accessed=8 * rows * width * 2,
            transcendentals=rows * heads,
        ),
    )(queries, keys, values, out_grad)


def solution(mesh):
    return jax.shard_map(
        body,
        mesh=mesh,
        in_specs=(P(("groups", "seq"), None),) * 4,
        out_specs=(P("seq", "groups", None),) + (P(("groups", "seq"), None),) * 3,
        check_vma=False,
    )
```

```python
import functools

import jax
import jax.numpy as jnp
from jax import lax
from jax.experimental import pallas as pl
from jax.experimental.pallas import tpu as pltpu
from jax.sharding import PartitionSpec as P

DH = 128
EPS = 1e-06
F32 = jnp.float32
BF16 = jnp.bfloat16
WIRE_LOCAL = jnp.bfloat16
WIRE_PLANE = jnp.bfloat16
UNROLL = 4
CHUNKS = 4


def dot(a, b, ca, cb):
    return lax.dot_general(a, b, (((ca,), (cb,)), ((), ())), preferred_element_type=F32)


def remote(src, dst, send_sem, recv_sem, device):
    return pltpu.make_async_remote_copy(
        src_ref=src,
        dst_ref=dst,
        send_sem=send_sem,
        recv_sem=recv_sem,
        device_id={"seq": device},
        device_id_type=pl.DeviceIdType.MESH,
    )


class Scan:
    def __init__(self, me, planes, members, share, forward, bufs):
        (self.mine, self.states, self.total, self.run, self.out2, self.in2, self.out3,
         self.result, self.s1, self.r1, self.s2, self.r2, self.s3, self.r3) = bufs
        self.planes, self.members, self.share, self.forward = planes, members, share, forward
        self.z, self.j = me // members, me % members
        self.zz = self.z if forward else planes - 1 - self.z
        self.levels = planes.bit_length() - 1

    def keep(self, h, value):
        self.mine[h] = value.astype(self.mine.dtype)

    def push(self, h):
        o, i = h // self.share, h % self.share

        @pl.when(o != self.j)
        def _():
            remote(self.mine.at[h], self.states.at[i, self.j], self.s1.at[h],
                   self.r1.at[i, self.j], self.z * self.members + o).start()

    def plane_device(self, zz):
        z = zz if self.forward else self.planes - 1 - zz
        return z * self.members + self.j

    def sends(self, level):
        return (self.zz & ((2 << level) - 1)) == (1 << level) - 1

    def up(self, level, i, d):
        return remote(self.out2.at[level, i], self.in2.at[level, i], self.s2.at[level, d, i],
                      self.r2.at[level, i], self.plane_device(self.zz + 1 + d))

    def start_level(self, level, i):
        @pl.when(self.sends(level))
        def _():
            value = self.total[i] if level == 0 else self.run[i] + self.total[i]
            self.out2[level, i] = value.astype(self.out2.dtype)
            for d in range(1 << level):
                self.up(level, i, d).start()

    def gather(self):
        for i in range(self.share):
            for s in range(1, self.members):
                o = self.j ^ s
                remote(self.mine.at[0], self.states.at[i, o], self.s1.at[0], self.r1.at[i, o],
                       self.z * self.members + o).wait_recv()
            self.states[i, self.j] = self.mine[self.j * self.share + i]
            total = self.states[i, 0].astype(F32)
            for o in range(1, self.members):
                total += self.states[i, o].astype(F32)
            self.total[i] = total
            self.run[i] = jnp.zeros_like(total)
            self.start_level(0, i)

    def spread(self):
        for i in range(self.share):
            for level in range(self.levels):
                if level:
                    self.start_level(level, i)

                @pl.when(((self.zz >> level) & 1) == 1)
                def _():
                    self.up(level, i, 0).wait_recv()
                    self.run[i] += self.in2[level, i].astype(F32)

            total = self.run[i]
            order = range(self.members) if self.forward else range(self.members - 1, -1, -1)
            h = self.j * self.share + i
            for o in order:
                rounded = total.astype(BF16)
                total += self.states[i, o].astype(F32)

                @pl.when(o == self.j)
                def _():
                    self.result[h] = rounded

                @pl.when(o != self.j)
                def _():
                    self.out3[i, o] = rounded
                    remote(self.out3.at[i, o], self.result.at[h], self.s3.at[i, o],
                           self.r3.at[h], self.z * self.members + o).start()

    def take(self, h):
        o = h // self.share

        @pl.when(o != self.j)
        def _():
            remote(self.out3.at[0, 0], self.result.at[h], self.s3.at[0, 0], self.r3.at[h],
                   self.z * self.members + o).wait_recv()

    def drain(self):
        for i in range(self.share):
            for s in range(1, self.members):
                o = self.j ^ s
                h = o * self.share + i
                remote(self.mine.at[h], self.states.at[i, self.j], self.s1.at[h],
                       self.r1.at[i, self.j], self.z * self.members + o).wait_send()
                remote(self.out3.at[i, o], self.result.at[h], self.s3.at[i, o], self.r3.at[h],
                       self.z * self.members + o).wait_send()
            for level in range(self.levels):
                @pl.when(self.sends(level))
                def _():
                    for d in range(1 << level):
                        self.up(level, i, d).wait_send()


def kernel(n, members, q_hbm, k_hbm, v_hbm, g_hbm, relaid, dq_hbm, dk_hbm, dv_hbm,
           q_ref, k_ref, v_ref, g_ref, dq_ref, dk_ref, dv_ref, score, intra, out, d_acc,
           dk_part, dv_part, in_sem, out_sem, own_sem, relaid_send, relaid_recv, *scans):
    me = lax.axis_index("seq")
    rows, width = q_ref.shape
    heads = width // DH
    planes, share = n // members, heads // members
    pieces = n // heads
    piece = rows // pieces
    fwd = Scan(me, planes, members, share, True, scans[: len(scans) // 2])
    bwd = Scan(me, planes, members, share, False, scans[len(scans) // 2:])

    loads = [
        pltpu.make_async_copy(src, dst, in_sem.at[x])
        for x, (src, dst) in enumerate(
            ((k_hbm, k_ref), (v_hbm, v_ref), (q_hbm, q_ref), (g_hbm, g_ref)))
    ]
    for load in loads:
        load.start()
    barrier = pltpu.get_barrier_semaphore()

    def greet(s, carry):
        pl.semaphore_signal(barrier, inc=1, device_id={"seq": lax.rem(me + s, n)},
                            device_id_type=pl.DeviceIdType.MESH)
        return carry

    lax.fori_loop(1, n, greet, 0)

    def cols(h):
        return pl.ds(pl.multiple_of(h * DH, DH), DH)

    loads[0].wait()
    loads[1].wait()
    pl.semaphore_wait(barrier, n - 1)

    def in_order(first, step):
        ts = [step * UNROLL + x for x in range(UNROLL)]
        return [(first ^ (members - 1 - t % members)) * share + t // members for t in ts]

    def local_step(step, carry):
        hs = in_order(fwd.j, step)
        for h in hs:
            fwd.keep(h, dot(k_ref[:, cols(h)], v_ref[:, cols(h)], 0, 0))
        for h in hs:
            fwd.push(h)
        return carry

    lax.fori_loop(0, heads // UNROLL, local_step, 0)
    loads[2].wait()
    causal = (lax.broadcasted_iota(jnp.int32, (rows, rows), 0)
              >= lax.broadcasted_iota(jnp.int32, (rows, rows), 1))

    def intra_step(h, carry):
        s = dot(q_ref[:, cols(h)], k_ref[:, cols(h)], 1, 1)
        s = jnp.where(causal, s, 0.0).astype(BF16)
        score[h] = s
        intra[h] = dot(s, v_ref[:, cols(h)], 1, 0)
        return carry

    lax.fori_loop(0, heads, intra_step, 0, unroll=UNROLL)
    loads[3].wait()
    fwd.gather()
    fwd.spread()

    def relaid_copy(h, p):
        return remote(out.at[h, pl.ds(p * piece, piece)],
                      relaid.at[0, pl.ds(pl.multiple_of(me * piece, 16), piece)],
                      relaid_send, relaid_recv, p * heads + h)

    def own_copy(p):
        return pltpu.make_async_copy(
            out.at[me % heads, pl.ds(pl.multiple_of(p * piece, 16), piece)],
            relaid.at[0, pl.ds(pl.multiple_of(me * piece, 16), piece)], own_sem)

    def main_step(step, carry):
        hs = in_order((me // members) % members, step)
        for h in hs:
            fwd.take(h)
        for h in hs:
            q = q_ref[:, cols(h)]
            acc = intra[h] + dot(q, fwd.result[h], 1, 0)
            inv = lax.rsqrt(jnp.mean(acc * acc, axis=-1, keepdims=True) + EPS)
            unit = acc * inv
            out[h] = unit.astype(BF16)
            g = g_ref[:, cols(h)].astype(F32)
            inner = jnp.mean(g * unit, axis=-1, keepdims=True)
            da = ((g - unit * inner) * inv).astype(BF16)
            d_acc[h] = da
            bwd.keep(h, dot(q, da, 0, 0))
        for h in hs:
            for p in range(pieces):
                @pl.when(p * heads + h != me)
                def _():
                    relaid_copy(h, p).start()
            bwd.push(h)
        return carry

    lax.fori_loop(0, heads // UNROLL, main_step, 0)
    own_copy(me // heads).start()

    def grad_step(h, carry):
        q, k, v = q_ref[:, cols(h)], k_ref[:, cols(h)], v_ref[:, cols(h)]
        da = d_acc[h]
        ds = dot(da, v, 1, 1)
        ds = jnp.where(causal, ds, 0.0).astype(BF16)
        dq_ref[:, cols(h)] = (dot(ds, k, 1, 0) + dot(da, fwd.result[h], 1, 1)).astype(BF16)
        dk_part[h] = dot(ds, q, 0, 0)
        dv_part[h] = dot(score[h], da, 0, 0)
        return carry

    lax.fori_loop(0, heads, grad_step, 0, unroll=UNROLL)
    dq_out = pltpu.make_async_copy(dq_ref, dq_hbm, out_sem.at[0])
    dq_out.start()
    bwd.gather()
    bwd.spread()

    def last_step(step, carry):
        hs = in_order(0, step)
        for h in hs:
            bwd.take(h)
        for h in hs:
            later = bwd.result[h]
            dk = dk_part[h] + dot(v_ref[:, cols(h)], later, 1, 1)
            dv = dv_part[h] + dot(k_ref[:, cols(h)], later, 1, 0)
            dk_ref[:, cols(h)] = dk.astype(BF16)
            dv_ref[:, cols(h)] = dv.astype(BF16)
        return carry

    lax.fori_loop(0, heads // UNROLL, last_step, 0)
    dk_out = pltpu.make_async_copy(dk_ref, dk_hbm, out_sem.at[1])
    dv_out = pltpu.make_async_copy(dv_ref, dv_hbm, out_sem.at[2])
    dk_out.start()
    dv_out.start()
    fwd.drain()
    bwd.drain()
    own_copy(me // heads).wait()
    whole = relaid.at[0, pl.ds(0, (n - 1) * piece)]
    pltpu.make_async_copy(whole, whole, relaid_send).wait()
    pltpu.make_async_copy(whole, whole, relaid_recv).wait()
    dq_out.wait()
    dk_out.wait()
    dv_out.wait()


def place(*refs):
    count = (len(refs) - 2) // 3
    srcs, dsts, held = refs[:count], refs[count : 2 * count], refs[2 * count : 3 * count]
    in_sem, out_sem = refs[-2:]
    loads, stores = [], []
    for x, (src, dst, buf) in enumerate(zip(srcs, dsts, held)):
        size = src.shape[0] // CHUNKS
        for c in range(CHUNKS):
            part = pl.ds(c * size, size)
            loads.append(pltpu.make_async_copy(src.at[part], buf.at[part], in_sem.at[x, c]))
            stores.append(pltpu.make_async_copy(buf.at[part], dst.at[part], out_sem.at[x, c]))
    for load in loads:
        load.start()
    for load, store in zip(loads, stores):
        load.wait()
        store.start()
    for store in stores:
        store.wait()


def body(queries, keys, values, out_grad):
    n = lax.axis_size("seq")
    rows, width = queries.shape
    heads = width // DH
    members = min(heads, n // 4 if n <= heads else n // 8)
    planes, share = n // members, heads // members
    levels = planes.bit_length() - 1
    piece = rows * heads // n
    dma = pltpu.SemaphoreType.DMA
    state = (DH, DH)
    scan = [
        pltpu.VMEM((heads,) + state, WIRE_LOCAL),
        pltpu.VMEM((share, members) + state, WIRE_LOCAL),
        pltpu.VMEM((share,) + state, F32),
        pltpu.VMEM((share,) + state, F32),
        pltpu.VMEM((levels, share) + state, WIRE_PLANE),
        pltpu.VMEM((levels, share) + state, WIRE_PLANE),
        pltpu.VMEM((share, members) + state, BF16),
        pltpu.VMEM((heads,) + state, BF16),
        dma((heads,)),
        dma((share, members)),
        dma((levels, 1 << (levels - 1), share)),
        dma((levels, share)),
        dma((share, members)),
        dma((heads,)),
    ]
    by_head = (heads, rows, DH)
    any_space = pl.BlockSpec(memory_space=pl.ANY)
    found = pl.pallas_call(
        functools.partial(kernel, n, members),
        out_shape=(
            jax.ShapeDtypeStruct((1, n * piece, DH), BF16),
            jax.ShapeDtypeStruct((rows, width), BF16),
            jax.ShapeDtypeStruct((rows, width), BF16),
            jax.ShapeDtypeStruct((rows, width), BF16),
        ),
        in_specs=[any_space] * 4,
        out_specs=(any_space,) * 4,
        scratch_shapes=[pltpu.VMEM((rows, width), BF16)] * 7
        + [
            pltpu.VMEM((heads, rows, rows), BF16),
            pltpu.VMEM(by_head, F32),
            pltpu.VMEM(by_head, BF16),
            pltpu.VMEM(by_head, BF16),
            pltpu.VMEM(by_head, F32),
            pltpu.VMEM(by_head, F32),
            dma((4,)),
            dma((3,)),
            dma,
            dma,
            dma,
        ]
        + scan
        + scan,
        compiler_params=pltpu.CompilerParams(
            collective_id=0, has_side_effects=True, vmem_limit_bytes=56 * 2**20
        ),
        cost_estimate=pl.CostEstimate(
            flops=heads * rows * DH * 12 * (rows + DH),
            bytes_accessed=8 * rows * width * 2,
            transcendentals=rows * heads,
        ),
    )(queries, keys, values, out_grad)
    flat = [x.reshape(-1, x.shape[-1]) for x in found]
    placed = pl.pallas_call(
        place,
        out_shape=tuple(jax.ShapeDtypeStruct(x.shape, x.dtype) for x in flat),
        in_specs=[any_space] * 4,
        out_specs=(any_space,) * 4,
        scratch_shapes=[pltpu.VMEM(x.shape, x.dtype) for x in flat]
        + [dma((len(flat), CHUNKS))] * 2,
        compiler_params=pltpu.CompilerParams(vmem_limit_bytes=56 * 2**20),
        cost_estimate=pl.CostEstimate(
            flops=0, bytes_accessed=16 * rows * width, transcendentals=0
        ),
    )(*flat)
    return (placed[0][None],) + tuple(placed[1:])


def solution(mesh):
    return jax.shard_map(
        body,
        mesh=mesh,
        in_specs=(P(("groups", "seq"), None),) * 4,
        out_specs=(P("seq", "groups", None),) + (P(("groups", "seq"), None),) * 3,
        check_vma=False,
    )
```

```python
import functools

import jax
import jax.numpy as jnp
from jax import lax
from jax.experimental import pallas as pl
from jax.experimental.pallas import tpu as pltpu
from jax.sharding import PartitionSpec as P

DH = 128
EPS = 1e-06
F32 = jnp.float32
BF16 = jnp.bfloat16
WIRE_LOCAL = jnp.bfloat16
WIRE_PLANE = jnp.bfloat16
UNROLL = 4
CHUNKS = 4


def dot(a, b, ca, cb):
    return lax.dot_general(a, b, (((ca,), (cb,)), ((), ())), preferred_element_type=F32)


def remote(src, dst, send_sem, recv_sem, device):
    return pltpu.make_async_remote_copy(
        src_ref=src,
        dst_ref=dst,
        send_sem=send_sem,
        recv_sem=recv_sem,
        device_id={"seq": device},
        device_id_type=pl.DeviceIdType.MESH,
    )


class Scan:
    def __init__(self, me, planes, members, share, forward, bufs):
        (self.mine, self.states, self.total, self.run, self.out2, self.in2, self.out3,
         self.result, self.s1, self.r1, self.s2, self.r2, self.s3, self.r3) = bufs
        self.planes, self.members, self.share, self.forward = planes, members, share, forward
        self.z, self.j = me // members, me % members
        self.zz = self.z if forward else planes - 1 - self.z
        self.levels = planes.bit_length() - 1

    def keep(self, h, value):
        self.mine[h] = value.astype(self.mine.dtype)

    def push(self, h):
        o, i = h // self.share, h % self.share

        @pl.when(o != self.j)
        def _():
            remote(self.mine.at[h], self.states.at[i, self.j], self.s1.at[h],
                   self.r1.at[i, self.j], self.z * self.members + o).start()

    def plane_device(self, zz):
        z = zz if self.forward else self.planes - 1 - zz
        return z * self.members + self.j

    def sends(self, level):
        return (self.zz & ((2 << level) - 1)) == (1 << level) - 1

    def up(self, level, i, d):
        return remote(self.out2.at[level, i], self.in2.at[level, i], self.s2.at[level, d, i],
                      self.r2.at[level, i], self.plane_device(self.zz + 1 + d))

    def start_level(self, level, i):
        @pl.when(self.sends(level))
        def _():
            value = self.total[i] if level == 0 else self.run[i] + self.total[i]
            self.out2[level, i] = value.astype(self.out2.dtype)
            for d in range(1 << level):
                self.up(level, i, d).start()

    def gather(self):
        for i in range(self.share):
            for s in range(1, self.members):
                o = self.j ^ s
                remote(self.mine.at[0], self.states.at[i, o], self.s1.at[0], self.r1.at[i, o],
                       self.z * self.members + o).wait_recv()
            self.states[i, self.j] = self.mine[self.j * self.share + i]
            total = self.states[i, 0].astype(F32)
            for o in range(1, self.members):
                total += self.states[i, o].astype(F32)
            self.total[i] = total
            self.run[i] = jnp.zeros_like(total)
            self.start_level(0, i)

    def spread(self):
        for i in range(self.share):
            for level in range(self.levels):
                if level:
                    self.start_level(level, i)

                @pl.when(((self.zz >> level) & 1) == 1)
                def _():
                    self.up(level, i, 0).wait_recv()
                    self.run[i] += self.in2[level, i].astype(F32)

            total = self.run[i]
            order = range(self.members) if self.forward else range(self.members - 1, -1, -1)
            h = self.j * self.share + i
            for o in order:
                rounded = total.astype(BF16)
                total += self.states[i, o].astype(F32)

                @pl.when(o == self.j)
                def _():
                    self.result[h] = rounded

                @pl.when(o != self.j)
                def _():
                    self.out3[i, o] = rounded
                    remote(self.out3.at[i, o], self.result.at[h], self.s3.at[i, o],
                           self.r3.at[h], self.z * self.members + o).start()

    def take(self, h):
        o = h // self.share

        @pl.when(o != self.j)
        def _():
            remote(self.out3.at[0, 0], self.result.at[h], self.s3.at[0, 0], self.r3.at[h],
                   self.z * self.members + o).wait_recv()

    def drain(self):
        for i in range(self.share):
            for s in range(1, self.members):
                o = self.j ^ s
                h = o * self.share + i
                remote(self.mine.at[h], self.states.at[i, self.j], self.s1.at[h],
                       self.r1.at[i, self.j], self.z * self.members + o).wait_send()
                remote(self.out3.at[i, o], self.result.at[h], self.s3.at[i, o], self.r3.at[h],
                       self.z * self.members + o).wait_send()
            for level in range(self.levels):
                @pl.when(self.sends(level))
                def _():
                    for d in range(1 << level):
                        self.up(level, i, d).wait_send()


def kernel(n, members, q_hbm, k_hbm, v_hbm, g_hbm, relaid, dq_hbm, dk_hbm, dv_hbm,
           q_ref, k_ref, v_ref, g_ref, dq_ref, dk_ref, dv_ref, score, intra, out, d_acc,
           dk_part, dv_part, in_sem, out_sem, own_sem, relaid_send, relaid_recv, *scans):
    me = lax.axis_index("seq")
    rows, width = q_ref.shape
    heads = width // DH
    planes, share = n // members, heads // members
    pieces = n // heads
    piece = rows // pieces
    fwd = Scan(me, planes, members, share, True, scans[: len(scans) // 2])
    bwd = Scan(me, planes, members, share, False, scans[len(scans) // 2:])

    loads = [
        pltpu.make_async_copy(src, dst, in_sem.at[x])
        for x, (src, dst) in enumerate(
            ((k_hbm, k_ref), (v_hbm, v_ref), (q_hbm, q_ref), (g_hbm, g_ref)))
    ]
    for load in loads:
        load.start()
    barrier = pltpu.get_barrier_semaphore()

    def greet(s, carry):
        pl.semaphore_signal(barrier, inc=1, device_id={"seq": lax.rem(me + s, n)},
                            device_id_type=pl.DeviceIdType.MESH)
        return carry

    lax.fori_loop(1, n, greet, 0)

    def cols(h):
        return pl.ds(pl.multiple_of(h * DH, DH), DH)

    loads[0].wait()
    loads[1].wait()
    pl.semaphore_wait(barrier, n - 1)

    def in_order(first, step):
        ts = [step * UNROLL + x for x in range(UNROLL)]
        return [(first ^ (members - 1 - t % members)) * share + t // members for t in ts]

    def local_step(step, carry):
        hs = in_order(fwd.j, step)
        for h in hs:
            fwd.keep(h, dot(k_ref[:, cols(h)], v_ref[:, cols(h)], 0, 0))
        for h in hs:
            fwd.push(h)
        return carry

    lax.fori_loop(0, heads // UNROLL, local_step, 0)
    loads[2].wait()
    causal = (lax.broadcasted_iota(jnp.int32, (rows, rows), 0)
              >= lax.broadcasted_iota(jnp.int32, (rows, rows), 1))

    def intra_step(h, carry):
        s = dot(q_ref[:, cols(h)], k_ref[:, cols(h)], 1, 1)
        s = jnp.where(causal, s, 0.0).astype(BF16)
        score[h] = s
        intra[h] = dot(s, v_ref[:, cols(h)], 1, 0)
        return carry

    lax.fori_loop(0, heads, intra_step, 0, unroll=2 * UNROLL)
    loads[3].wait()
    fwd.gather()
    fwd.spread()

    def relaid_copy(h, p):
        return remote(out.at[h, pl.ds(p * piece, piece)],
                      relaid.at[0, pl.ds(pl.multiple_of(me * piece, 16), piece)],
                      relaid_send, relaid_recv, p * heads + h)

    def own_copy(p):
        return pltpu.make_async_copy(
            out.at[me % heads, pl.ds(pl.multiple_of(p * piece, 16), piece)],
            relaid.at[0, pl.ds(pl.multiple_of(me * piece, 16), piece)], own_sem)

    def main_step(step, carry):
        hs = in_order((me // members) % members, step)
        for h in hs:
            fwd.take(h)
        for h in hs:
            q = q_ref[:, cols(h)]
            acc = intra[h] + dot(q, fwd.result[h], 1, 0)
            inv = lax.rsqrt(jnp.mean(acc * acc, axis=-1, keepdims=True) + EPS)
            unit = acc * inv
            out[h] = unit.astype(BF16)
            g = g_ref[:, cols(h)].astype(F32)
            inner = jnp.mean(g * unit, axis=-1, keepdims=True)
            da = ((g - unit * inner) * inv).astype(BF16)
            d_acc[h] = da
            bwd.keep(h, dot(q, da, 0, 0))
        for h in hs:
            for p in range(pieces):
                @pl.when(p * heads + h != me)
                def _():
                    relaid_copy(h, p).start()
            bwd.push(h)
        return carry

    lax.fori_loop(0, heads // UNROLL, main_step, 0)
    own_copy(me // heads).start()

    def grad_step(h, carry):
        q, k, v = q_ref[:, cols(h)], k_ref[:, cols(h)], v_ref[:, cols(h)]
        da = d_acc[h]
        ds = dot(da, v, 1, 1)
        ds = jnp.where(causal, ds, 0.0).astype(BF16)
        dq_ref[:, cols(h)] = (dot(ds, k, 1, 0) + dot(da, fwd.result[h], 1, 1)).astype(BF16)
        dk_part[h] = dot(ds, q, 0, 0)
        dv_part[h] = dot(score[h], da, 0, 0)
        return carry

    lax.fori_loop(0, heads, grad_step, 0, unroll=2 * UNROLL)
    dq_out = pltpu.make_async_copy(dq_ref, dq_hbm, out_sem.at[0])
    dq_out.start()
    bwd.gather()
    bwd.spread()

    def last_step(step, carry):
        hs = in_order(0, step)
        for h in hs:
            bwd.take(h)
        for h in hs:
            later = bwd.result[h]
            dk = dk_part[h] + dot(v_ref[:, cols(h)], later, 1, 1)
            dv = dv_part[h] + dot(k_ref[:, cols(h)], later, 1, 0)
            dk_ref[:, cols(h)] = dk.astype(BF16)
            dv_ref[:, cols(h)] = dv.astype(BF16)
        return carry

    lax.fori_loop(0, heads // UNROLL, last_step, 0)
    dk_out = pltpu.make_async_copy(dk_ref, dk_hbm, out_sem.at[1])
    dv_out = pltpu.make_async_copy(dv_ref, dv_hbm, out_sem.at[2])
    dk_out.start()
    dv_out.start()
    fwd.drain()
    bwd.drain()
    own_copy(me // heads).wait()
    whole = relaid.at[0, pl.ds(0, (n - 1) * piece)]
    pltpu.make_async_copy(whole, whole, relaid_send).wait()
    pltpu.make_async_copy(whole, whole, relaid_recv).wait()
    dq_out.wait()
    dk_out.wait()
    dv_out.wait()


def place(*refs):
    count = (len(refs) - 2) // 3
    srcs, dsts, held = refs[:count], refs[count : 2 * count], refs[2 * count : 3 * count]
    in_sem, out_sem = refs[-2:]
    loads, stores = [], []
    for x, (src, dst, buf) in enumerate(zip(srcs, dsts, held)):
        size = src.shape[0] // CHUNKS
        for c in range(CHUNKS):
            part = pl.ds(c * size, size)
            loads.append(pltpu.make_async_copy(src.at[part], buf.at[part], in_sem.at[x, c]))
            stores.append(pltpu.make_async_copy(buf.at[part], dst.at[part], out_sem.at[x, c]))
    for load in loads:
        load.start()
    for load, store in zip(loads, stores):
        load.wait()
        store.start()
    for store in stores:
        store.wait()


def body(queries, keys, values, out_grad):
    n = lax.axis_size("seq")
    rows, width = queries.shape
    heads = width // DH
    members = min(heads, n // 4 if n <= heads else n // 8)
    planes, share = n // members, heads // members
    levels = planes.bit_length() - 1
    piece = rows * heads // n
    dma = pltpu.SemaphoreType.DMA
    state = (DH, DH)
    scan = [
        pltpu.VMEM((heads,) + state, WIRE_LOCAL),
        pltpu.VMEM((share, members) + state, WIRE_LOCAL),
        pltpu.VMEM((share,) + state, F32),
        pltpu.VMEM((share,) + state, F32),
        pltpu.VMEM((levels, share) + state, WIRE_PLANE),
        pltpu.VMEM((levels, share) + state, WIRE_PLANE),
        pltpu.VMEM((share, members) + state, BF16),
        pltpu.VMEM((heads,) + state, BF16),
        dma((heads,)),
        dma((share, members)),
        dma((levels, 1 << (levels - 1), share)),
        dma((levels, share)),
        dma((share, members)),
        dma((heads,)),
    ]
    by_head = (heads, rows, DH)
    any_space = pl.BlockSpec(memory_space=pl.ANY)
    found = pl.pallas_call(
        functools.partial(kernel, n, members),
        out_shape=(
            jax.ShapeDtypeStruct((1, n * piece, DH), BF16),
            jax.ShapeDtypeStruct((rows, width), BF16),
            jax.ShapeDtypeStruct((rows, width), BF16),
            jax.ShapeDtypeStruct((rows, width), BF16),
        ),
        in_specs=[any_space] * 4,
        out_specs=(any_space,) * 4,
        scratch_shapes=[pltpu.VMEM((rows, width), BF16)] * 7
        + [
            pltpu.VMEM((heads, rows, rows), BF16),
            pltpu.VMEM(by_head, F32),
            pltpu.VMEM(by_head, BF16),
            pltpu.VMEM(by_head, BF16),
            pltpu.VMEM(by_head, F32),
            pltpu.VMEM(by_head, F32),
            dma((4,)),
            dma((3,)),
            dma,
            dma,
            dma,
        ]
        + scan
        + scan,
        compiler_params=pltpu.CompilerParams(
            collective_id=0, has_side_effects=True, vmem_limit_bytes=56 * 2**20
        ),
        cost_estimate=pl.CostEstimate(
            flops=heads * rows * DH * 12 * (rows + DH),
            bytes_accessed=8 * rows * width * 2,
            transcendentals=rows * heads,
        ),
    )(queries, keys, values, out_grad)
    flat = [x.reshape(-1, x.shape[-1]) for x in found]
    placed = pl.pallas_call(
        place,
        out_shape=tuple(jax.ShapeDtypeStruct(x.shape, x.dtype) for x in flat),
        in_specs=[any_space] * 4,
        out_specs=(any_space,) * 4,
        scratch_shapes=[pltpu.VMEM(x.shape, x.dtype) for x in flat]
        + [dma((len(flat), CHUNKS))] * 2,
        compiler_params=pltpu.CompilerParams(vmem_limit_bytes=56 * 2**20),
        cost_estimate=pl.CostEstimate(
            flops=0, bytes_accessed=16 * rows * width, transcendentals=0
        ),
    )(*flat)
    return (placed[0][None],) + tuple(placed[1:])


def solution(mesh):
    return jax.shard_map(
        body,
        mesh=mesh,
        in_specs=(P(("groups", "seq"), None),) * 4,
        out_specs=(P("seq", "groups", None),) + (P(("groups", "seq"), None),) * 3,
        check_vma=False,
    )
```
